128 devices in a mesh: lat: 64 (over x, y, z), lev: 2 (over core).
Axes of the slice: x: 4, y: 4, z: 4, core: 2. Of those that a mesh axis runs over, the one named last changes fastest.
Arguments:
- fourier: bfloat16 [640, 2, 4, 16, 1536], P('lat', None, None, 'lev'), may hold values from -6 to 6
- vertical_band: float32 [4, 16, 5], replicated, may hold values from -3 to 3
- cycle_points: int32 [640], P('lat'), may hold values from 20 to 3091
- legendre: bfloat16 [768, 2, 640, 640], P(('lat', 'lev')), may hold values from -0.25 to 0.25
- wave_of_slot: int32 [768], replicated, may hold values from 0 to 767, as said below
Outputs:
- spectral: bfloat16 [768, 2, 640, 128], P(('lat', 'lev'))
The draws below stay inside these ranges and needn't reach their ends.
Inputs may be any that keep to these rules, and one draw needn't show every extreme that they name: A permutation of the wavenumbers: slot q of legendre and spectral belongs to wavenumber wave_of_slot[q]. The device runs of 6 slots take wavenumbers dealt in rounds of alternating direction. Wavenumber m is resolved on the cycles of pair j where 2 m < cycle_points[j].
All inputs are finite; a program needn't handle non-finite values.
Results may differ from the reference program's by a relative error of at most 0.001.
Values may be sent and summed in bfloat16 or wider, within the bound.
No kernel may reach another device: no remote copies, remote signals or barrier semaphores. Data moves between devices by JAX's collectives and lax.ppermute only.
A program may use at most 320 MiB of HBM per device.

```python
import jax
import jax.numpy as jnp
from jax import lax

FIELDS = 4
NPAIR = 640
NW = 768
NT = 1280
LEV = 16
BW = 2
KH = 640
SLOTS = 6


def draw_wave_of_slot(key, part):
    holders = NW // SLOTS
    order = jax.random.permutation(key, holders).astype(jnp.int32)
    rounds = jnp.arange(SLOTS, dtype=jnp.int32)
    forward = rounds[None, :] * holders + order[:, None]
    backward = rounds[None, :] * holders + (holders - 1 - order[:, None])
    waves = jnp.where(rounds[None, :] % 2 == 0, forward, backward)
    return waves.reshape(NW).astype(jnp.int32)


def touch_ends(values, own_key, smallest, largest):
    longest = values.shape.index(max(values.shape))
    spots = []
    for shift in (0, 1):
        where = [jax.random.randint(jax.random.fold_in(own_key, axis), (), 0, length) for axis, length in enumerate(values.shape)]
        where[longest] = (where[longest] + shift) % values.shape[longest]
        spots.append(tuple(where))
    return values.at[spots[0]].set(smallest).at[spots[1]].set(largest)


def block_scale(own_key, dims, cuts, least, largest):
    loudness = 1.0
    for dim, blocks in cuts:
        draws = jax.random.uniform(jax.random.fold_in(jax.random.fold_in(own_key, 6), dim), (blocks,), jnp.float32, least / len(cuts), largest / len(cuts))
        loudness = loudness * jnp.repeat(jnp.exp(draws), dims[dim] // blocks).reshape((-1,) + (1,) * (len(dims) - 1 - dim))
    return loudness


def noise(own_key, shape, width, limit, cuts=(), kind=jnp.bfloat16):
    gain = block_scale(own_key, shape, cuts, -0.22, 0.18) if cuts else 1.0
    drawn = jax.random.normal(own_key, shape, jnp.float32) * width * gain
    return jnp.minimum(jnp.maximum(drawn, -limit), limit).astype(kind)


def setup_inputs(seed: int = 0) -> dict:
    arg_keys = jax.random.split(jax.random.key(seed), 6)
    fourier = noise(arg_keys[0], (NPAIR, 2, FIELDS, LEV, 2 * NW), 1.0, 6.0, ((0, 64), (3, 2)))
    vertical_band = noise(arg_keys[1], (FIELDS, LEV, 2 * BW + 1), 0.45, 3.0, (), jnp.float32)
    cycle_points = touch_ends(jax.random.randint(arg_keys[2], (NPAIR,), 20, 4 * NW + 20), jax.random.fold_in(arg_keys[2], 1), 20, (4 * NW + 20) - 1).astype(jnp.int32)
    legendre = noise(arg_keys[3], (NW, 2, KH, NPAIR), NPAIR ** -0.5, 0.25, ((0, 128),))
    wave_of_slot = draw_wave_of_slot(jax.random.fold_in(arg_keys[5], 71), 0)
    return {"fourier": fourier, "vertical_band": vertical_band, "cycle_points": cycle_points, "legendre": legendre, "wave_of_slot": wave_of_slot}


def reference(fourier, vertical_band, cycle_points, legendre, wave_of_slot):
    reach = BW
    band_padded = jnp.pad(vertical_band, ((0, 0), (reach, reach), (0, 0)))
    column_wave = jnp.arange(2 * NW, dtype=jnp.int32) % NW

    def fold_pair(item):
        cycles, points = item
        padded = jnp.pad(cycles.astype(jnp.float32), ((0, 0), (0, 0), (reach, reach), (0, 0)))
        vertical = jnp.zeros(cycles.shape, jnp.float32)
        for offset in range(2 * reach + 1):
            first = 2 * reach - offset
            weights = band_padded[:, first:first + LEV, offset]
            vertical = vertical + weights[None, :, :, None] * padded[:, :, first:first + LEV, :]
        keep = (2 * column_wave < points).astype(jnp.float32)
        masked = vertical * keep
        return jnp.stack([masked[0] + masked[1], masked[0] - masked[1]])

    folded = lax.map(fold_pair, (fourier, cycle_points))
    split = folded.reshape(NPAIR, 2, FIELDS, LEV, 2, NW)
    ordered = jnp.take(split, wave_of_slot.astype(jnp.int32), axis=5)
    ordered = jnp.transpose(ordered, (5, 1, 0, 2, 3, 4)).reshape(NW, 2, NPAIR, FIELDS * LEV * 2)
    degree_rows = jnp.arange(KH, dtype=jnp.int32)
    parity = jnp.arange(2, dtype=jnp.int32)[:, None]

    def transform(item):
        table, right, wave = item
        product = jnp.einsum("skj,sjc->skc", table.astype(jnp.float32), right, precision=lax.Precision.HIGHEST)
        valid = wave + 2 * degree_rows[None, :] + parity < NT
        return jnp.where(valid[:, :, None], product, 0.0).astype(jnp.bfloat16)

    return lax.map(transform, (legendre, ordered, wave_of_slot.astype(jnp.int32)))
```

```python
import functools

import jax
import jax.numpy as jnp
import numpy as np
from jax import lax
from jax.experimental import pallas as pl
from jax.experimental.pallas import tpu as pltpu
from jax.sharding import PartitionSpec as P

NT_DIMS = (((1,), (1,)), ((), ()))


def pack_kernel(fourier_ref, cycles_ref, wave_ref, out_ref, pick_ref, column_ref, rows_ref, *, lev, slots):
    pairs, parts, waves = fourier_ref.shape[0], 2, fourier_ref.shape[2] // 2
    holders = waves // slots
    lat = holders // lev
    for i in range(waves // 128):
        line = jnp.broadcast_to(wave_ref[pl.ds(i, 1), :], (128, 128))
        column_ref[pl.ds(i * 128, 128), :] = line.T
    lane = lax.broadcasted_iota(jnp.int32, (lat, 128), 1)
    for q in range(slots):
        for v in range(lev):
            column = column_ref[pl.ds(v * slots + q, lat, stride=lev * slots), :]
            for b in range(waves // 128):
                hit = jnp.where(column == lane + b * 128, 1.0, 0.0).astype(jnp.bfloat16)
                pick_ref[pl.ds((q * lev + v) * lat, lat), pl.ds(b * 128, 128)] = hit
    wave = lax.broadcasted_iota(jnp.int32, (1, waves), 1)
    run = pairs * slots
    for j in range(0, pairs, 2):
        blocks = []
        for i in (j, j + 1):
            keep = 2 * wave < cycles_ref[i]
            for r in range(parts):
                part = fourier_ref[i, :, pl.ds(r * waves, waves)]
                blocks.append(jnp.where(keep, part, jnp.zeros_like(part)))
        block = jnp.concatenate(blocks, axis=0)
        for q in range(slots):
            picked = lax.dot_general(
                pick_ref[pl.ds(q * holders, holders), :], block, NT_DIMS,
                preferred_element_type=jnp.float32,
            )
            for i in range(2):
                rows_ref[pl.ds((j + i) * slots + q, holders, stride=run), :] = picked[:, i * 128:(i + 1) * 128]
    out_ref[...] = rows_ref[...].astype(jnp.bfloat16)


def split_bf16(value):
    high = value.astype(jnp.bfloat16)
    low = (value - high.astype(jnp.float32)).astype(jnp.bfloat16)
    return high, low


def transform_kernel(wave_ref, arrived_ref, vertical_ref, table_ref, out_ref,
                     arrived, tables, folded, result, arrived_sem, table_sem, out_sem, *, lev, limit):
    slots, sides, rows, pairs = tables.shape
    half = arrived.shape[0] // lev
    arrive = pltpu.make_async_copy(arrived_ref, arrived, arrived_sem)
    arrive.start()
    for q in range(slots):
        for s in range(sides):
            pltpu.make_async_copy(table_ref.at[q, s], tables.at[q, s], table_sem.at[q, s]).start()
    v_high, v_low = split_bf16(vertical_ref[...])
    arrive.wait()
    step = 480

    @pl.loop(0, half // step)
    def _(i):
        at = pl.multiple_of(i * step, step)
        source = jnp.concatenate([arrived[pl.ds(v * half + at, step), :] for v in range(lev)], axis=1)
        made = jnp.dot(source, v_high, preferred_element_type=jnp.float32)
        made = made + jnp.dot(source, v_low, preferred_element_type=jnp.float32)
        for s in range(sides):
            folded[s, pl.ds(at, step), :] = made[:, s * 128:(s + 1) * 128]

    degree = 2 * lax.broadcasted_iota(jnp.int32, (rows, 128), 0)

    @pl.loop(0, slots)
    def _(q):
        for s in range(sides):
            column = folded[s, pl.ds(q, pairs, stride=slots), :]
            right = jnp.concatenate(split_bf16(column), axis=1)
            pltpu.make_async_copy(table_ref.at[q, s], tables.at[q, s], table_sem.at[q, s]).wait()
            both = jnp.dot(tables[q, s], right, preferred_element_type=jnp.float32)
            product = both[:, :128] + both[:, 128:]
            valid = degree < limit - s - wave_ref[q]
            result[q, s] = jnp.where(valid, product, 0.0).astype(jnp.bfloat16)
            pltpu.make_async_copy(result.at[q, s], out_ref.at[q, s], out_sem.at[q, s]).start()

    for q in range(slots):
        for s in range(sides):
            pltpu.make_async_copy(result.at[q, s], out_ref.at[q, s], out_sem.at[q, s]).wait()


def vertical_matrix(band, lev):
    fields, levels, width = band.shape
    reach = (width - 1) // 2
    here = levels // lev
    source = band.reshape(fields, lev, here, width).transpose(1, 0, 2, 3)[:, None, None]
    source = jnp.broadcast_to(source, (lev, 2, 2, fields, here, width)).reshape(-1, width)
    row = np.arange(source.shape[0])[:, None]
    column = np.arange(source.shape[0])[None, :]
    row_level = row // (4 * fields * here) * here + row % here
    row_group = row // (2 * fields * here) % 2 * fields + row // here % fields
    group = column % 2 * fields + column // (2 * levels) % fields
    offset = np.where(row_group == group, column // 2 % levels - row_level + reach, width).astype(np.int8)
    sign = np.where((row // (here * fields) % 2 == 1) & (column // (2 * levels * fields) == 1), -1, 1).astype(np.int8)
    value = jnp.zeros(offset.shape, jnp.float32)
    for d in range(width):
        value = jnp.where(offset == d, source[:, d:d + 1], value)
    return value * sign


def pack(fourier, cycle_points, wave_of_slot, lev, slots):
    pairs, sides, fields, here, columns = fourier.shape
    waves = columns // 2
    holders = waves // slots
    lanes = sides * fields * here
    return pl.pallas_call(
        functools.partial(pack_kernel, lev=lev, slots=slots),
        out_shape=jax.ShapeDtypeStruct((waves * pairs, 2 * lanes), jnp.bfloat16),
        in_specs=[
            pl.BlockSpec(memory_space=pltpu.VMEM),
            pl.BlockSpec(memory_space=pltpu.SMEM),
            pl.BlockSpec(memory_space=pltpu.VMEM),
        ],
        out_specs=pl.BlockSpec(memory_space=pltpu.VMEM),
        scratch_shapes=[
            pltpu.VMEM((waves, waves), jnp.bfloat16),
            pltpu.VMEM((waves, 128), jnp.int32),
            pltpu.VMEM((waves * pairs, 2 * lanes), jnp.float32),
        ],
        compiler_params=pltpu.CompilerParams(vmem_limit_bytes=40 * 1024 * 1024),
        name="pack",
    )(fourier.reshape(pairs, lanes, columns), cycle_points, wave_of_slot.reshape(waves // 128, 128))


def transform(own_waves, arrived, vertical, legendre, lev):
    slots, sides, rows, pairs = legendre.shape
    total, lanes = arrived.shape
    any_space = pl.BlockSpec(memory_space=pl.ANY)
    return pl.pallas_call(
        functools.partial(transform_kernel, lev=lev, limit=2 * rows),
        out_shape=jax.ShapeDtypeStruct((slots, sides, rows, lanes), jnp.bfloat16),
        in_specs=[
            pl.BlockSpec(memory_space=pltpu.SMEM),
            any_space,
            pl.BlockSpec(memory_space=pltpu.VMEM),
            any_space,
        ],
        out_specs=any_space,
        scratch_shapes=[
            pltpu.VMEM((total, lanes), jnp.bfloat16),
            pltpu.VMEM((slots, sides, rows, pairs), jnp.bfloat16),
            pltpu.VMEM((sides, total // lev, lanes), jnp.float32),
            pltpu.VMEM((slots, sides, rows, lanes), jnp.bfloat16),
            pltpu.SemaphoreType.DMA,
            pltpu.SemaphoreType.DMA((slots, sides)),
            pltpu.SemaphoreType.DMA((slots, sides)),
        ],
        compiler_params=pltpu.CompilerParams(vmem_limit_bytes=40 * 1024 * 1024),
        name="transform",
    )(own_waves, arrived, vertical, legendre)


def body(fourier, vertical_band, cycle_points, legendre, wave_of_slot):
    slots = legendre.shape[0]
    lat, lev = lax.axis_size("lat"), lax.axis_size("lev")
    outgoing = pack(fourier, cycle_points, wave_of_slot, lev, slots)
    split = outgoing.reshape(lat * lev, outgoing.shape[0] // (lat * lev * 4), 4, outgoing.shape[1])
    arrived = lax.all_to_all(split, ("lev", "lat"), split_axis=0, concat_axis=0, tiled=True)
    vertical_band, waves = lax.optimization_barrier((vertical_band, wave_of_slot, outgoing))[:2]
    own_waves = lax.dynamic_slice_in_dim(waves, lax.axis_index(("lat", "lev")) * slots, slots)
    vertical = vertical_matrix(vertical_band, lev)
    return transform(own_waves, arrived.reshape(outgoing.shape), vertical, legendre, lev)


def solution(mesh):
    in_specs = (
        P("lat", None, None, "lev", None),
        P(),
        P("lat"),
        P(("lat", "lev"), None, None, None),
        P(),
    )
    out_specs = P(("lat", "lev"), None, None, None)
    return jax.shard_map(body, mesh=mesh, in_specs=in_specs, out_specs=out_specs, check_vma=False)
```

```python
import functools

import jax
import jax.numpy as jnp
import numpy as np
from jax import lax
from jax.experimental import pallas as pl
from jax.experimental.pallas import tpu as pltpu
from jax.sharding import PartitionSpec as P

NT_DIMS = (((1,), (1,)), ((), ()))


def pack_kernel(cycles_ref, fourier_ref, wave_ref, out_ref,
                fourier, wave, pick, column_ref, rows_ref, packed, in_sem, wave_sem, out_sem, *, lev, slots):
    pairs, parts, waves = fourier_ref.shape[0], 2, fourier_ref.shape[2] // 2
    holders = waves // slots
    lat = holders // lev
    run = pairs * slots
    group = 2

    def arriving(j):
        return pltpu.make_async_copy(fourier_ref.at[pl.ds(j, group)], fourier.at[pl.ds(j, group)], in_sem.at[j // group])

    arrive_wave = pltpu.make_async_copy(wave_ref, wave, wave_sem)
    arrive_wave.start()
    for j in range(0, pairs, group):
        arriving(j).start()
    arrive_wave.wait()
    shape = (waves // 128, 128)
    slot = lax.rem(lax.broadcasted_iota(jnp.int32, shape, 0) * 128 + lax.broadcasted_iota(jnp.int32, shape, 1), slots)
    dealt = jnp.max(jnp.abs(lax.shift_right_logical(wave[...], 7) - slot)) == 0
    for i in range(waves // 128):
        column_ref[pl.ds(i * 128, 128), :] = jnp.broadcast_to(wave[pl.ds(i, 1), :], (128, 128)).T
    lane = lax.broadcasted_iota(jnp.int32, (lat, 128), 1)

    def fill(blocks_of):
        for q in range(slots):
            for v in range(lev):
                column = column_ref[pl.ds(v * slots + q, lat, stride=lev * slots), :]
                for b in blocks_of(q):
                    hit = jnp.where(column == lane + b * 128, 1.0, 0.0).astype(jnp.bfloat16)
                    pick[pl.ds((q * lev + v) * lat, lat), pl.ds(b * 128, 128)] = hit

    index = lax.broadcasted_iota(jnp.int32, (1, waves), 1)

    def gather(columns_of):
        for j in range(0, pairs, group):
            arriving(j).wait()
            blocks = []
            for i in range(j, j + group):
                keep = 2 * index < cycles_ref[i]
                for r in range(parts):
                    part = fourier[i, :, pl.ds(r * waves, waves)]
                    blocks.append(jnp.where(keep, part, jnp.zeros_like(part)))
            block = jnp.concatenate(blocks, axis=0)
            for q in range(slots):
                first, last = columns_of(q)
                picked = lax.dot_general(
                    pick[pl.ds(q * holders, holders), first:last], block[:, first:last], NT_DIMS,
                    preferred_element_type=jnp.float32,
                )
                for i in range(group):
                    rows_ref[pl.ds((j + i) * slots + q, holders, stride=run), :] = picked[:, i * 128:(i + 1) * 128]

    @pl.when(dealt)
    def _():
        fill(lambda q: [q])
        gather(lambda q: (q * 128, (q + 1) * 128))

    @pl.when(jnp.logical_not(dealt))
    def _():
        fill(lambda q: range(waves // 128))
        gather(lambda q: (0, waves))

    chunks = out_sem.shape[0]
    step = packed.shape[0] // chunks

    def leaving(i):
        part = pl.ds(i * step, step)
        return pltpu.make_async_copy(packed.at[part], out_ref.at[part], out_sem.at[i])

    for i in range(chunks):
        packed[pl.ds(i * step, step), :] = rows_ref[pl.ds(i * step, step), :].astype(jnp.bfloat16)
        leaving(i).start()
    for i in range(chunks):
        leaving(i).wait()


def split_bf16(value):
    high = value.astype(jnp.bfloat16)
    low = (value - high.astype(jnp.float32)).astype(jnp.bfloat16)
    return high, low


def transform_kernel(wave_ref, arrived_ref, vertical_ref, table_ref, out_ref,
                     arrived, vertical, tables, folded, right, result, in_sem, vertical_sem, table_sem, out_sem,
                     *, lev, limit):
    slots, sides, rows, pairs = tables.shape
    half = arrived.shape[0] // lev
    chunks = in_sem.shape[0]
    step = half // chunks
    tile = 128
    counts = range(rows // tile // 2 + 1, rows // tile + 1)

    def arriving(i, v):
        part = pl.ds(v * half + i * step, step)
        return pltpu.make_async_copy(arrived_ref.at[part], arrived.at[part], in_sem.at[i, v])

    def table(q, n):
        part = pl.ds(0, n * tile)
        return pltpu.make_async_copy(table_ref.at[q, :, part], tables.at[q, :, part], table_sem.at[q])

    def count(q):
        return jnp.clip((limit - wave_ref[q] + 2 * tile - 1) // (2 * tile), counts[0], counts[-1])

    def start_table(q):
        for n in counts:
            @pl.when(count(q) == n)
            def _():
                table(q, n).start()

    upper = pltpu.make_async_copy(vertical_ref, vertical, vertical_sem)
    upper.start()
    for i in range(chunks):
        for v in range(lev):
            arriving(i, v).start()
    upper.wait()
    ready = 0
    sent = 0
    for i in range(chunks):
        while ready < min(chunks, i + chunks // 2):
            for v in range(lev):
                arriving(ready, v).wait()
            ready += 1
        while sent < slots * ready // chunks:
            start_table(sent)
            sent += 1
        at = i * step
        source = jnp.concatenate([arrived[pl.ds(v * half + at, step), :] for v in range(lev)] * 2, axis=1)
        made = jnp.dot(source, vertical[...], preferred_element_type=jnp.float32)
        for s in range(sides):
            folded[s, pl.ds(at, step), :] = made[:, s * 128:(s + 1) * 128]

    degree = 2 * lax.broadcasted_iota(jnp.int32, (tile, 128), 0)

    def prepare(q, s):
        column = folded[s, pl.ds(q, pairs, stride=slots), :]
        right[s][...] = jnp.concatenate(split_bf16(column), axis=1)

    prepare(0, 0)

    @pl.loop(0, slots)
    def _(q):
        for n in counts:
            @pl.when(count(q) == n)
            def _():
                table(q, n).wait()
                for s in range(sides):
                    prepare(q, 1) if s == 0 else prepare(jnp.minimum(q + 1, slots - 1), 0)
                    for i in range(n):
                        part = pl.ds(i * tile, tile)
                        both = jnp.dot(tables[q, s, part], right[s][...], preferred_element_type=jnp.float32)
                        product = both[:, :128] + both[:, 128:]
                        valid = degree < limit - 2 * i * tile - s - wave_ref[q]
                        result[q, s, part] = jnp.where(valid, product, 0.0).astype(jnp.bfloat16)
                    if n * tile < rows:
                        rest = pl.ds(n * tile, rows - n * tile)
                        result[q, s, rest] = jnp.zeros((rows - n * tile, 128), jnp.bfloat16)
        pltpu.make_async_copy(result.at[q], out_ref.at[q], out_sem.at[q]).start()

    for q in range(slots):
        pltpu.make_async_copy(result.at[q], out_ref.at[q], out_sem.at[q]).wait()


def vertical_matrix(band, lev):
    fields, levels, width = band.shape
    reach = (width - 1) // 2
    here = levels // lev
    source = band.reshape(fields, lev, here, width).transpose(1, 0, 2, 3)[:, None, None]
    source = jnp.broadcast_to(source, (lev, 2, 2, fields, here, width)).reshape(-1, width)
    row = np.arange(source.shape[0])[:, None]
    column = np.arange(source.shape[0])[None, :]
    row_level = row // (4 * fields * here) * here + row % here
    row_group = row // (2 * fields * here) % 2 * fields + row // here % fields
    group = column % 2 * fields + column // (2 * levels) % fields
    offset = np.where(row_group == group, column // 2 % levels - row_level + reach, width).astype(np.int8)
    sign = np.where((row // (here * fields) % 2 == 1) & (column // (2 * levels * fields) == 1), -1, 1).astype(np.int8)
    value = jnp.zeros(offset.shape, jnp.float32)
    for d in range(width):
        value = jnp.where(offset == d, source[:, d:d + 1], value)
    value = value * sign
    high = lax.reduce_precision(value, 8, 7)
    return jnp.concatenate([high, value - high], axis=0).astype(jnp.bfloat16)


def pack(fourier, cycle_points, wave_of_slot, lev, slots):
    pairs, sides, fields, here, columns = fourier.shape
    waves = columns // 2
    lanes = sides * fields * here
    any_space = pl.BlockSpec(memory_space=pl.ANY)
    return pl.pallas_call(
        functools.partial(pack_kernel, lev=lev, slots=slots),
        out_shape=jax.ShapeDtypeStruct((waves * pairs, 2 * lanes), jnp.bfloat16),
        in_specs=[pl.BlockSpec(memory_space=pltpu.SMEM), any_space, any_space],
        out_specs=any_space,
        scratch_shapes=[
            pltpu.VMEM((pairs, lanes, columns), jnp.bfloat16),
            pltpu.VMEM((waves // 128, 128), jnp.int32),
            pltpu.VMEM((waves, waves), jnp.bfloat16),
            pltpu.VMEM((waves, 128), jnp.int32),
            pltpu.VMEM((waves * pairs, 2 * lanes), jnp.float32),
            pltpu.VMEM((waves * pairs, 2 * lanes), jnp.bfloat16),
            pltpu.SemaphoreType.DMA((pairs // 2,)),
            pltpu.SemaphoreType.DMA,
            pltpu.SemaphoreType.DMA((4,)),
        ],
        compiler_params=pltpu.CompilerParams(vmem_limit_bytes=60 * 1024 * 1024),
        name="pack",
    )(cycle_points, fourier.reshape(pairs, lanes, columns), wave_of_slot.reshape(waves // 128, 128))


def transform(own_waves, arrived, vertical, legendre, lev):
    slots, sides, rows, pairs = legendre.shape
    total, lanes = arrived.shape
    any_space = pl.BlockSpec(memory_space=pl.ANY)
    return pl.pallas_call(
        functools.partial(transform_kernel, lev=lev, limit=2 * rows),
        out_shape=jax.ShapeDtypeStruct((slots, sides, rows, lanes), jnp.bfloat16),
        in_specs=[
            pl.BlockSpec(memory_space=pltpu.SMEM),
            any_space,
            any_space,
            any_space,
        ],
        out_specs=any_space,
        scratch_shapes=[
            pltpu.VMEM((total, lanes), jnp.bfloat16),
            pltpu.VMEM(vertical.shape, jnp.bfloat16),
            pltpu.VMEM((slots, sides, rows, pairs), jnp.bfloat16),
            pltpu.VMEM((sides, total // lev, lanes), jnp.float32),
            [pltpu.VMEM((pairs, 2 * lanes), jnp.bfloat16)] * sides,
            pltpu.VMEM((slots, sides, rows, lanes), jnp.bfloat16),
            pltpu.SemaphoreType.DMA((4, lev)),
            pltpu.SemaphoreType.DMA,
            pltpu.SemaphoreType.DMA((slots,)),
            pltpu.SemaphoreType.DMA((slots,)),
        ],
        compiler_params=pltpu.CompilerParams(vmem_limit_bytes=60 * 1024 * 1024),
        name="transform",
    )(own_waves, arrived, vertical, legendre)


def body(fourier, vertical_band, cycle_points, legendre, wave_of_slot):
    slots = legendre.shape[0]
    lat, lev = lax.axis_size("lat"), lax.axis_size("lev")
    outgoing = pack(fourier, cycle_points, wave_of_slot, lev, slots)
    split = outgoing.reshape(lat * lev, outgoing.shape[0] // (lat * lev * 4), 4, outgoing.shape[1])
    arrived = lax.all_to_all(split, ("lev", "lat"), split_axis=0, concat_axis=0, tiled=True)
    vertical_band, waves = lax.optimization_barrier((vertical_band, wave_of_slot, outgoing))[:2]
    own_waves = lax.dynamic_slice_in_dim(waves, lax.axis_index(("lat", "lev")) * slots, slots)
    vertical = vertical_matrix(vertical_band, lev)
    return transform(own_waves, arrived.reshape(outgoing.shape), vertical, legendre, lev)


def solution(mesh):
    in_specs = (
        P("lat", None, None, "lev", None),
        P(),
        P("lat"),
        P(("lat", "lev"), None, None, None),
        P(),
    )
    out_specs = P(("lat", "lev"), None, None, None)
    return jax.shard_map(body, mesh=mesh, in_specs=in_specs, out_specs=out_specs, check_vma=False)
```

```python
import functools

import jax
import jax.numpy as jnp
import numpy as np
from jax import lax
from jax.experimental import pallas as pl
from jax.experimental.pallas import tpu as pltpu
from jax.sharding import PartitionSpec as P

NT_DIMS = (((1,), (1,)), ((), ()))


def pack_kernel(cycles_ref, fourier_ref, wave_ref, out_ref,
                fourier, wave, pick, column_ref, rows_ref, in_sem, wave_sem, *, lev, slots):
    pairs, parts, waves = fourier_ref.shape[0], 2, fourier_ref.shape[2] // 2
    holders = waves // slots
    lat = holders // lev
    run = pairs * slots
    group = 2

    def arriving(j):
        return pltpu.make_async_copy(fourier_ref.at[pl.ds(j, group)], fourier.at[pl.ds(j, group)], in_sem.at[j // group])

    arrive_wave = pltpu.make_async_copy(wave_ref, wave, wave_sem)
    arrive_wave.start()
    for j in range(0, pairs, group):
        arriving(j).start()
    arrive_wave.wait()
    shape = (waves // 128, 128)
    slot = lax.rem(lax.broadcasted_iota(jnp.int32, shape, 0) * 128 + lax.broadcasted_iota(jnp.int32, shape, 1), slots)
    dealt = jnp.max(jnp.abs(lax.shift_right_logical(wave[...], 7) - slot)) == 0
    for i in range(waves // 128):
        column_ref[pl.ds(i * 128, 128), :] = jnp.broadcast_to(wave[pl.ds(i, 1), :], (128, 128)).T
    lane = lax.broadcasted_iota(jnp.int32, (lat, 128), 1)

    def fill(blocks_of):
        for q in range(slots):
            for v in range(lev):
                column = column_ref[pl.ds(v * slots + q, lat, stride=lev * slots), :]
                for b in blocks_of(q):
                    hit = jnp.where(column == lane + b * 128, 1.0, 0.0).astype(jnp.bfloat16)
                    pick[pl.ds((q * lev + v) * lat, lat), pl.ds(b * 128, 128)] = hit

    index = lax.broadcasted_iota(jnp.int32, (1, waves), 1)

    def gather(columns_of):
        for j in range(0, pairs, group):
            arriving(j).wait()
            blocks = []
            for i in range(j, j + group):
                keep = 2 * index < cycles_ref[i]
                for r in range(parts):
                    part = fourier[i, :, pl.ds(r * waves, waves)]
                    blocks.append(jnp.where(keep, part, jnp.zeros_like(part)))
            block = jnp.concatenate(blocks, axis=0)
            for q in range(slots):
                first, last = columns_of(q)
                picked = lax.dot_general(
                    pick[pl.ds(q * holders, holders), first:last], block[:, first:last], NT_DIMS,
                    preferred_element_type=jnp.float32,
                )
                for i in range(group):
                    rows_ref[pl.ds((j + i) * slots + q, holders, stride=run), :] = picked[:, i * 128:(i + 1) * 128]

    @pl.when(dealt)
    def _():
        fill(lambda q: [q])
        gather(lambda q: (q * 128, (q + 1) * 128))

    @pl.when(jnp.logical_not(dealt))
    def _():
        fill(lambda q: range(waves // 128))
        gather(lambda q: (0, waves))

    out_ref[...] = rows_ref[...].astype(jnp.bfloat16)


def split_bf16(value):
    high = value.astype(jnp.bfloat16)
    low = (value - high.astype(jnp.float32)).astype(jnp.bfloat16)
    return high, low


def transform_kernel(wave_ref, arrived, vertical, table_ref, out_ref,
                     tables, folded, right, result, table_sem, out_sem, *, lev, limit):
    slots, sides, rows, pairs = tables.shape
    half = arrived.shape[0] // lev
    chunks = 4
    step = half // chunks
    tile = 128
    counts = range(rows // tile // 2 + 1, rows // tile + 1)

    def table(q, n):
        part = pl.ds(0, n * tile)
        return pltpu.make_async_copy(table_ref.at[q, :, part], tables.at[q, :, part], table_sem.at[q])

    def count(q):
        return jnp.clip((limit - wave_ref[q] + 2 * tile - 1) // (2 * tile), counts[0], counts[-1])

    def start_table(q):
        for n in counts:
            @pl.when(count(q) == n)
            def _():
                table(q, n).start()

    for q in range(slots):
        start_table(q)
    for i in range(chunks):
        at = i * step
        source = jnp.concatenate([arrived[pl.ds(v * half + at, step), :] for v in range(lev)] * 2, axis=1)
        made = jnp.dot(source, vertical[...], preferred_element_type=jnp.float32)
        for s in range(sides):
            folded[s, pl.ds(at, step), :] = made[:, s * 128:(s + 1) * 128]

    degree = 2 * lax.broadcasted_iota(jnp.int32, (tile, 128), 0)

    def prepare(q, s):
        column = folded[s, pl.ds(q, pairs, stride=slots), :]
        right[s][...] = jnp.concatenate(split_bf16(column), axis=1)

    prepare(0, 0)

    @pl.loop(0, slots)
    def _(q):
        for n in counts:
            @pl.when(count(q) == n)
            def _():
                table(q, n).wait()
                for s in range(sides):
                    prepare(q, 1) if s == 0 else prepare(jnp.minimum(q + 1, slots - 1), 0)
                    for i in range(n):
                        part = pl.ds(i * tile, tile)
                        both = jnp.dot(tables[q, s, part], right[s][...], preferred_element_type=jnp.float32)
                        product = both[:, :128] + both[:, 128:]
                        valid = degree < limit - 2 * i * tile - s - wave_ref[q]
                        result[q, s, part] = jnp.where(valid, product, 0.0).astype(jnp.bfloat16)
                    if n * tile < rows:
                        rest = pl.ds(n * tile, rows - n * tile)
                        result[q, s, rest] = jnp.zeros((rows - n * tile, 128), jnp.bfloat16)
        pltpu.make_async_copy(result.at[q], out_ref.at[q], out_sem.at[q]).start()

    for q in range(slots):
        pltpu.make_async_copy(result.at[q], out_ref.at[q], out_sem.at[q]).wait()


def vertical_matrix(band, lev):
    fields, levels, width = band.shape
    reach = (width - 1) // 2
    here = levels // lev
    source = band.reshape(fields, lev, here, width).transpose(1, 0, 2, 3)[:, None, None]
    source = jnp.broadcast_to(source, (lev, 2, 2, fields, here, width)).reshape(-1, width)
    row = np.arange(source.shape[0])[:, None]
    column = np.arange(source.shape[0])[None, :]
    row_level = row // (4 * fields * here) * here + row % here
    row_group = row // (2 * fields * here) % 2 * fields + row // here % fields
    group = column % 2 * fields + column // (2 * levels) % fields
    offset = np.where(row_group == group, column // 2 % levels - row_level + reach, width).astype(np.int8)
    sign = np.where((row // (here * fields) % 2 == 1) & (column // (2 * levels * fields) == 1), -1, 1).astype(np.int8)
    value = jnp.zeros(offset.shape, jnp.float32)
    for d in range(width):
        value = jnp.where(offset == d, source[:, d:d + 1], value)
    value = value * sign
    high = lax.reduce_precision(value, 8, 7)
    return jnp.concatenate([high, value - high], axis=0).astype(jnp.bfloat16)


def pack(fourier, cycle_points, wave_of_slot, lev, slots):
    pairs, sides, fields, here, columns = fourier.shape
    waves = columns // 2
    lanes = sides * fields * here
    any_space = pl.BlockSpec(memory_space=pl.ANY)
    return pl.pallas_call(
        functools.partial(pack_kernel, lev=lev, slots=slots),
        out_shape=jax.ShapeDtypeStruct((waves * pairs, 2 * lanes), jnp.bfloat16),
        in_specs=[pl.BlockSpec(memory_space=pltpu.SMEM), any_space, any_space],
        out_specs=pl.BlockSpec(memory_space=pltpu.VMEM),
        scratch_shapes=[
            pltpu.VMEM((pairs, lanes, columns), jnp.bfloat16),
            pltpu.VMEM((waves // 128, 128), jnp.int32),
            pltpu.VMEM((waves, waves), jnp.bfloat16),
            pltpu.VMEM((waves, 128), jnp.int32),
            pltpu.VMEM((waves * pairs, 2 * lanes), jnp.float32),
            pltpu.SemaphoreType.DMA((pairs // 2,)),
            pltpu.SemaphoreType.DMA,
        ],
        compiler_params=pltpu.CompilerParams(vmem_limit_bytes=60 * 1024 * 1024),
        name="pack",
    )(cycle_points, fourier.reshape(pairs, lanes, columns), wave_of_slot.reshape(waves // 128, 128))


def transform(own_waves, arrived, vertical, legendre, lev):
    slots, sides, rows, pairs = legendre.shape
    total, lanes = arrived.shape
    any_space = pl.BlockSpec(memory_space=pl.ANY)
    return pl.pallas_call(
        functools.partial(transform_kernel, lev=lev, limit=2 * rows),
        out_shape=jax.ShapeDtypeStruct((slots, sides, rows, lanes), jnp.bfloat16),
        in_specs=[
            pl.BlockSpec(memory_space=pltpu.SMEM),
            pl.BlockSpec(memory_space=pltpu.VMEM),
            pl.BlockSpec(memory_space=pltpu.VMEM),
            any_space,
        ],
        out_specs=any_space,
        scratch_shapes=[
            pltpu.VMEM((slots, sides, rows, pairs), jnp.bfloat16),
            pltpu.VMEM((sides, total // lev, lanes), jnp.float32),
            [pltpu.VMEM((pairs, 2 * lanes), jnp.bfloat16)] * sides,
            pltpu.VMEM((slots, sides, rows, lanes), jnp.bfloat16),
            pltpu.SemaphoreType.DMA((slots,)),
            pltpu.SemaphoreType.DMA((slots,)),
        ],
        compiler_params=pltpu.CompilerParams(vmem_limit_bytes=50 * 1024 * 1024),
        name="transform",
    )(own_waves, arrived, vertical, legendre)


def body(fourier, vertical_band, cycle_points, legendre, wave_of_slot):
    slots = legendre.shape[0]
    lat, lev = lax.axis_size("lat"), lax.axis_size("lev")
    outgoing = pack(fourier, cycle_points, wave_of_slot, lev, slots)
    split = outgoing.reshape(lat * lev, outgoing.shape[0] // (lat * lev * 4), 4, outgoing.shape[1])
    arrived = lax.all_to_all(split, ("lev", "lat"), split_axis=0, concat_axis=0, tiled=True)
    vertical_band, waves = lax.optimization_barrier((vertical_band, wave_of_slot, outgoing))[:2]
    own_waves = lax.dynamic_slice_in_dim(waves, lax.axis_index(("lat", "lev")) * slots, slots)
    vertical = vertical_matrix(vertical_band, lev)
    return transform(own_waves, arrived.reshape(outgoing.shape), vertical, legendre, lev)


def solution(mesh):
    in_specs = (
        P("lat", None, None, "lev", None),
        P(),
        P("lat"),
        P(("lat", "lev"), None, None, None),
        P(),
    )
    out_specs = P(("lat", "lev"), None, None, None)
    return jax.shard_map(body, mesh=mesh, in_specs=in_specs, out_specs=out_specs, check_vma=False)
```

```python
import functools

import jax
import jax.numpy as jnp
import numpy as np
from jax import lax
from jax.experimental import pallas as pl
from jax.experimental.pallas import tpu as pltpu
from jax.sharding import PartitionSpec as P

NT_DIMS = (((1,), (1,)), ((), ()))


def pack_kernel(cycles_ref, fourier_ref, wave_ref, out_ref,
                fourier, wave, pick, column_ref, rows_ref, in_sem, wave_sem, *, lev, slots):
    pairs, parts, waves = fourier_ref.shape[0], 2, fourier_ref.shape[2] // 2
    holders = waves // slots
    lat = holders // lev
    run = pairs * slots
    group = 2

    arrive = pltpu.make_async_copy(fourier_ref, fourier, in_sem)
    arrive.start()
    arrive_wave = pltpu.make_async_copy(wave_ref, wave, wave_sem)
    arrive_wave.start()
    arrive_wave.wait()
    shape = (waves // 128, 128)
    slot = lax.rem(lax.broadcasted_iota(jnp.int32, shape, 0) * 128 + lax.broadcasted_iota(jnp.int32, shape, 1), slots)
    dealt = jnp.max(jnp.abs(lax.shift_right_logical(wave[...], 7) - slot)) == 0
    for i in range(waves // 128):
        column_ref[pl.ds(i * 128, 128), :] = jnp.broadcast_to(wave[pl.ds(i, 1), :], (128, 128)).T
    lane = lax.broadcasted_iota(jnp.int32, (lat, 128), 1)

    def fill(blocks_of):
        for q in range(slots):
            for v in range(lev):
                column = column_ref[pl.ds(v * slots + q, lat, stride=lev * slots), :]
                for b in blocks_of(q):
                    hit = jnp.where(column == lane + b * 128, 1.0, 0.0).astype(jnp.bfloat16)
                    pick[pl.ds((q * lev + v) * lat, lat), pl.ds(b * 128, 128)] = hit

    index = lax.broadcasted_iota(jnp.int32, (1, waves), 1)

    def gather(columns_of):
        arrive.wait()
        for j in range(0, pairs, group):
            blocks = []
            for i in range(j, j + group):
                keep = 2 * index < cycles_ref[i]
                for r in range(parts):
                    part = fourier[i, :, pl.ds(r * waves, waves)]
                    blocks.append(jnp.where(keep, part, jnp.zeros_like(part)))
            block = jnp.concatenate(blocks, axis=0)
            for q in range(slots):
                first, last = columns_of(q)
                picked = lax.dot_general(
                    pick[pl.ds(q * holders, holders), first:last], block[:, first:last], NT_DIMS,
                    preferred_element_type=jnp.float32,
                )
                for i in range(group):
                    rows_ref[pl.ds((j + i) * slots + q, holders, stride=run), :] = picked[:, i * 128:(i + 1) * 128]

    @pl.when(dealt)
    def _():
        fill(lambda q: [q])
        gather(lambda q: (q * 128, (q + 1) * 128))

    @pl.when(jnp.logical_not(dealt))
    def _():
        fill(lambda q: range(waves // 128))
        gather(lambda q: (0, waves))

    out_ref[...] = rows_ref[...].astype(jnp.bfloat16)


def split_bf16(value):
    high = value.astype(jnp.bfloat16)
    low = (value - high.astype(jnp.float32)).astype(jnp.bfloat16)
    return high, low


def transform_kernel(wave_ref, arrived, vertical, table_ref, out_ref,
                     tables, folded, right, result, table_sem, out_sem, *, lev, block, limit):
    slots, sides, rows, pairs = tables.shape
    half = arrived.shape[0] // lev
    step = half // 4
    tile = 128

    def table(q, n):
        part = pl.ds(0, n * tile)
        return pltpu.make_async_copy(table_ref.at[q, :, part], tables.at[q, :, part], table_sem.at[q])

    def leaving(q):
        return pltpu.make_async_copy(result.at[q], out_ref.at[q], out_sem.at[q])

    def fold():
        for at in range(0, half, step):
            source = jnp.concatenate([arrived[pl.ds(v * half + at, step), :] for v in range(lev)] * 2, axis=1)
            made = jnp.dot(source, vertical[...], preferred_element_type=jnp.float32)
            for s in range(sides):
                folded[s, pl.ds(at, step), :] = made[:, s * 128:(s + 1) * 128]

    degree = 2 * lax.broadcasted_iota(jnp.int32, (tile, 128), 0)

    def prepare(q, s):
        column = folded[s, pl.ds(q, pairs, stride=slots), :]
        right[s][...] = jnp.concatenate(split_bf16(column), axis=1)

    def multiply(q, s, n):
        for i in range(n):
            part = pl.ds(i * tile, tile)
            both = jnp.dot(tables[q, s, part], right[s][...], preferred_element_type=jnp.float32)
            product = both[:, :128] + both[:, 128:]
            valid = degree < limit - 2 * i * tile - s - wave_ref[q]
            result[q, s, part] = jnp.where(valid, product, 0.0).astype(jnp.bfloat16)
        if n * tile < rows:
            result[q, s, pl.ds(n * tile, rows - n * tile)] = jnp.zeros((rows - n * tile, 128), jnp.bfloat16)

    counts = [min(rows // tile, -(-(limit - q * block) // (2 * tile))) for q in range(slots)]
    fits = wave_ref[0] >= 0
    for q in range(1, slots):
        fits = jnp.logical_and(fits, wave_ref[q] >= q * block)
    groups = {0: (0,), 1: (1, 2), 3: (3, 4, 5)}

    @pl.when(fits)
    def _():
        for q in range(slots):
            table(q, counts[q]).start()
        fold()
        prepare(0, 0)
        for q in range(slots):
            for k in groups.get(q, ()):
                table(k, counts[k]).wait()
            for s in range(sides):
                after = q + (s + 1) // sides
                if after < slots:
                    prepare(after, (s + 1) % sides)
                multiply(q, s, counts[q])
            leaving(q).start()
        for q in range(slots):
            leaving(q).wait()

    @pl.when(jnp.logical_not(fits))
    def _():
        for q in range(slots):
            table(q, rows // tile).start()
        fold()

        @pl.loop(0, slots)
        def _(q):
            table(q, rows // tile).wait()
            for s in range(sides):
                prepare(q, s)
                multiply(q, s, rows // tile)
            leaving(q).start()

        for q in range(slots):
            leaving(q).wait()


def vertical_matrix(band, lev):
    fields, levels, width = band.shape
    reach = (width - 1) // 2
    here = levels // lev
    source = band.reshape(fields, lev, here, width).transpose(1, 0, 2, 3)[:, None, None]
    source = jnp.broadcast_to(source, (lev, 2, 2, fields, here, width)).reshape(-1, width)
    row = np.arange(source.shape[0])[:, None]
    column = np.arange(source.shape[0])[None, :]
    row_level = row // (4 * fields * here) * here + row % here
    row_group = row // (2 * fields * here) % 2 * fields + row // here % fields
    group = column % 2 * fields + column // (2 * levels) % fields
    offset = np.where(row_group == group, column // 2 % levels - row_level + reach, width).astype(np.int8)
    sign = np.where((row // (here * fields) % 2 == 1) & (column // (2 * levels * fields) == 1), -1, 1).astype(np.int8)
    value = jnp.zeros(offset.shape, jnp.float32)
    for d in range(width):
        value = jnp.where(offset == d, source[:, d:d + 1], value)
    value = value * sign
    high = lax.reduce_precision(value, 8, 7)
    return jnp.concatenate([high, value - high], axis=0).astype(jnp.bfloat16)


def pack(fourier, cycle_points, wave_of_slot, lev, slots):
    pairs, sides, fields, here, columns = fourier.shape
    waves = columns // 2
    lanes = sides * fields * here
    any_space = pl.BlockSpec(memory_space=pl.ANY)
    return pl.pallas_call(
        functools.partial(pack_kernel, lev=lev, slots=slots),
        out_shape=jax.ShapeDtypeStruct((waves * pairs, 2 * lanes), jnp.bfloat16),
        in_specs=[pl.BlockSpec(memory_space=pltpu.SMEM), any_space, any_space],
        out_specs=pl.BlockSpec(memory_space=pltpu.VMEM),
        scratch_shapes=[
            pltpu.VMEM((pairs, lanes, columns), jnp.bfloat16),
            pltpu.VMEM((waves // 128, 128), jnp.int32),
            pltpu.VMEM((waves, waves), jnp.bfloat16),
            pltpu.VMEM((waves, 128), jnp.int32),
            pltpu.VMEM((waves * pairs, 2 * lanes), jnp.float32),
            pltpu.SemaphoreType.DMA,
            pltpu.SemaphoreType.DMA,
        ],
        compiler_params=pltpu.CompilerParams(vmem_limit_bytes=60 * 1024 * 1024),
        name="pack",
    )(cycle_points, fourier.reshape(pairs, lanes, columns), wave_of_slot.reshape(waves // 128, 128))


def transform(own_waves, arrived, vertical, legendre, lev, block=128):
    slots, sides, rows, pairs = legendre.shape
    total, lanes = arrived.shape
    any_space = pl.BlockSpec(memory_space=pl.ANY)
    return pl.pallas_call(
        functools.partial(transform_kernel, lev=lev, block=block, limit=2 * rows),
        out_shape=jax.ShapeDtypeStruct((slots, sides, rows, lanes), jnp.bfloat16),
        in_specs=[
            pl.BlockSpec(memory_space=pltpu.SMEM),
            pl.BlockSpec(memory_space=pltpu.VMEM),
            pl.BlockSpec(memory_space=pltpu.VMEM),
            any_space,
        ],
        out_specs=any_space,
        scratch_shapes=[
            pltpu.VMEM((slots, sides, rows, pairs), jnp.bfloat16),
            pltpu.VMEM((sides, total // lev, lanes), jnp.float32),
            [pltpu.VMEM((pairs, 2 * lanes), jnp.bfloat16)] * sides,
            pltpu.VMEM((slots, sides, rows, lanes), jnp.bfloat16),
            pltpu.SemaphoreType.DMA((slots,)),
            pltpu.SemaphoreType.DMA((slots,)),
        ],
        compiler_params=pltpu.CompilerParams(vmem_limit_bytes=50 * 1024 * 1024),
        name="transform",
    )(own_waves, arrived, vertical, legendre)


def body(fourier, vertical_band, cycle_points, legendre, wave_of_slot):
    slots = legendre.shape[0]
    lat, lev = lax.axis_size("lat"), lax.axis_size("lev")
    outgoing = pack(fourier, cycle_points, wave_of_slot, lev, slots)
    split = outgoing.reshape(lat * lev, outgoing.shape[0] // (lat * lev * 4), 4, outgoing.shape[1])
    arrived = lax.all_to_all(split, ("lev", "lat"), split_axis=0, concat_axis=0, tiled=True)
    vertical_band, waves = lax.optimization_barrier((vertical_band, wave_of_slot, outgoing))[:2]
    own_waves = lax.dynamic_slice_in_dim(waves, lax.axis_index(("lat", "lev")) * slots, slots)
    vertical = vertical_matrix(vertical_band, lev)
    return transform(own_waves, arrived.reshape(outgoing.shape), vertical, legendre, lev, lat * lev)


def solution(mesh):
    in_specs = (
        P("lat", None, None, "lev", None),
        P(),
        P("lat"),
        P(("lat", "lev"), None, None, None),
        P(),
    )
    out_specs = P(("lat", "lev"), None, None, None)
    return jax.shard_map(body, mesh=mesh, in_specs=in_specs, out_specs=out_specs, check_vma=False)
```

```python
import functools

import jax
import jax.numpy as jnp
import numpy as np
from jax import lax
from jax.experimental import pallas as pl
from jax.experimental.pallas import tpu as pltpu
from jax.sharding import PartitionSpec as P

NT_DIMS = (((1,), (1,)), ((), ()))


def pack_kernel(cycles_ref, fourier_ref, wave_ref, out_ref,
                fourier, wave, pick, column_ref, rows_ref, packed, in_sem, wave_sem, out_sem, *, lev, slots):
    pairs, parts, waves = fourier_ref.shape[0], 2, fourier_ref.shape[2] // 2
    holders = waves // slots
    lat = holders // lev
    run = pairs * slots
    group = 2

    arrive = pltpu.make_async_copy(fourier_ref, fourier, in_sem)
    arrive.start()
    arrive_wave = pltpu.make_async_copy(wave_ref, wave, wave_sem)
    arrive_wave.start()
    arrive_wave.wait()
    shape = (waves // 128, 128)
    slot = lax.rem(lax.broadcasted_iota(jnp.int32, shape, 0) * 128 + lax.broadcasted_iota(jnp.int32, shape, 1), slots)
    dealt = jnp.max(jnp.abs(lax.shift_right_logical(wave[...], 7) - slot)) == 0
    for i in range(waves // 128):
        column_ref[pl.ds(i * 128, 128), :] = jnp.broadcast_to(wave[pl.ds(i, 1), :], (128, 128)).T
    lane = lax.broadcasted_iota(jnp.int32, (lat, 128), 1)

    def fill(blocks_of):
        for q in range(slots):
            for v in range(lev):
                column = column_ref[pl.ds(v * slots + q, lat, stride=lev * slots), :]
                for b in blocks_of(q):
                    hit = jnp.where(column == lane + b * 128, 1.0, 0.0).astype(jnp.bfloat16)
                    pick[pl.ds((q * lev + v) * lat, lat), pl.ds(b * 128, 128)] = hit

    index = lax.broadcasted_iota(jnp.int32, (1, waves), 1)

    def gather(columns_of):
        arrive.wait()
        for j in range(0, pairs, group):
            blocks = []
            for i in range(j, j + group):
                keep = 2 * index < cycles_ref[i]
                for r in range(parts):
                    part = fourier[i, :, pl.ds(r * waves, waves)]
                    blocks.append(jnp.where(keep, part, jnp.zeros_like(part)))
            block = jnp.concatenate(blocks, axis=0)
            for q in range(slots):
                first, last = columns_of(q)
                picked = lax.dot_general(
                    pick[pl.ds(q * holders, holders), first:last], block[:, first:last], NT_DIMS,
                    preferred_element_type=jnp.float32,
                )
                for i in range(group):
                    rows_ref[pl.ds((j + i) * slots + q, holders, stride=run), :] = picked[:, i * 128:(i + 1) * 128]

    @pl.when(dealt)
    def _():
        fill(lambda q: [q])
        gather(lambda q: (q * 128, (q + 1) * 128))

    @pl.when(jnp.logical_not(dealt))
    def _():
        fill(lambda q: range(waves // 128))
        gather(lambda q: (0, waves))

    part = packed.shape[0] // out_sem.shape[0]

    def leaving(i):
        at = pl.ds(i * part, part)
        return pltpu.make_async_copy(packed.at[at], out_ref.at[at], out_sem.at[i])

    for i in range(out_sem.shape[0]):
        packed[pl.ds(i * part, part), :] = rows_ref[pl.ds(i * part, part), :].astype(jnp.bfloat16)
        leaving(i).start()
    for i in range(out_sem.shape[0]):
        leaving(i).wait()


def split_bf16(value):
    high = value.astype(jnp.bfloat16)
    low = (value - high.astype(jnp.float32)).astype(jnp.bfloat16)
    return high, low


def transform_kernel(wave_ref, arrived, vertical, table_ref, out_ref,
                     tables, folded, right, result, table_sem, out_sem, *, lev, block, limit):
    slots, sides, rows, pairs = tables.shape
    half = arrived.shape[0] // lev
    step = half // 8
    tile = 128

    def table(q, n):
        part = pl.ds(0, n * tile)
        return pltpu.make_async_copy(table_ref.at[q, :, part], tables.at[q, :, part], table_sem.at[q])

    def leaving(q):
        return pltpu.make_async_copy(result.at[q], out_ref.at[q], out_sem.at[q])

    def fold():
        for at in range(0, half, step):
            source = jnp.concatenate([arrived[pl.ds(v * half + at, step), :] for v in range(lev)] * 2, axis=1)
            made = jnp.dot(source, vertical[...], preferred_element_type=jnp.float32)
            for s in range(sides):
                folded[s, pl.ds(at, step), :] = made[:, s * 128:(s + 1) * 128]

    degree = 2 * lax.broadcasted_iota(jnp.int32, (rows, 128), 0)

    def prepare(q, s):
        column = folded[s, pl.ds(q, pairs, stride=slots), :]
        right[s][...] = jnp.concatenate(split_bf16(column), axis=1)

    def multiply(q, s, n):
        size = n * tile
        for at in range(0, n * tile, size):
            part = pl.ds(at, size)
            both = jnp.dot(tables[q, s, part], right[s][...], preferred_element_type=jnp.float32)
            product = both[:, :128] + both[:, 128:]
            valid = degree[:size] < limit - 2 * at - s - wave_ref[q]
            result[q, s, part] = jnp.where(valid, product, 0.0).astype(jnp.bfloat16)
        if n * tile < rows:
            result[q, s, pl.ds(n * tile, rows - n * tile)] = jnp.zeros((rows - n * tile, 128), jnp.bfloat16)

    counts = [min(rows // tile, -(-(limit - q * block) // (2 * tile))) for q in range(slots)]
    fits = wave_ref[0] >= 0
    for q in range(1, slots):
        fits = jnp.logical_and(fits, wave_ref[q] >= q * block)
    groups = {0: (0,), 1: (1, 2), 3: (3, 4, 5)}

    @pl.when(fits)
    def _():
        for q in range(slots):
            table(q, counts[q]).start()
        fold()
        prepare(0, 0)
        for q in range(slots):
            for k in groups.get(q, ()):
                table(k, counts[k]).wait()
            for s in range(sides):
                after = q + (s + 1) // sides
                if after < slots:
                    prepare(after, (s + 1) % sides)
                multiply(q, s, counts[q])
            leaving(q).start()
        for q in range(slots):
            leaving(q).wait()

    @pl.when(jnp.logical_not(fits))
    def _():
        for q in range(slots):
            table(q, rows // tile).start()
        fold()

        @pl.loop(0, slots)
        def _(q):
            table(q, rows // tile).wait()
            for s in range(sides):
                prepare(q, s)
                multiply(q, s, rows // tile)
            leaving(q).start()

        for q in range(slots):
            leaving(q).wait()


def vertical_matrix(band, lev):
    fields, levels, width = band.shape
    reach = (width - 1) // 2
    here = levels // lev
    source = band.reshape(fields, lev, here, width).transpose(1, 0, 2, 3)[:, None, None]
    source = jnp.broadcast_to(source, (lev, 2, 2, fields, here, width)).reshape(-1, width)
    row = np.arange(source.shape[0])[:, None]
    column = np.arange(source.shape[0])[None, :]
    row_level = row // (4 * fields * here) * here + row % here
    row_group = row // (2 * fields * here) % 2 * fields + row // here % fields
    group = column % 2 * fields + column // (2 * levels) % fields
    offset = np.where(row_group == group, column // 2 % levels - row_level + reach, width).astype(np.int8)
    sign = np.where((row // (here * fields) % 2 == 1) & (column // (2 * levels * fields) == 1), -1, 1).astype(np.int8)
    value = jnp.zeros(offset.shape, jnp.float32)
    for d in range(width):
        value = jnp.where(offset == d, source[:, d:d + 1], value)
    value = value * sign
    high = lax.reduce_precision(value, 8, 7)
    return jnp.concatenate([high, value - high], axis=0).astype(jnp.bfloat16)


def pack(fourier, cycle_points, wave_of_slot, lev, slots):
    pairs, sides, fields, here, columns = fourier.shape
    waves = columns // 2
    lanes = sides * fields * here
    any_space = pl.BlockSpec(memory_space=pl.ANY)
    return pl.pallas_call(
        functools.partial(pack_kernel, lev=lev, slots=slots),
        out_shape=jax.ShapeDtypeStruct((waves * pairs, 2 * lanes), jnp.bfloat16),
        in_specs=[pl.BlockSpec(memory_space=pltpu.SMEM), any_space, any_space],
        out_specs=any_space,
        scratch_shapes=[
            pltpu.VMEM((pairs, lanes, columns), jnp.bfloat16),
            pltpu.VMEM((waves // 128, 128), jnp.int32),
            pltpu.VMEM((waves, waves), jnp.bfloat16),
            pltpu.VMEM((waves, 128), jnp.int32),
            pltpu.VMEM((waves * pairs, 2 * lanes), jnp.float32),
            pltpu.VMEM((waves * pairs, 2 * lanes), jnp.bfloat16),
            pltpu.SemaphoreType.DMA,
            pltpu.SemaphoreType.DMA,
            pltpu.SemaphoreType.DMA((2,)),
        ],
        compiler_params=pltpu.CompilerParams(vmem_limit_bytes=60 * 1024 * 1024),
        name="pack",
    )(cycle_points, fourier.reshape(pairs, lanes, columns), wave_of_slot.reshape(waves // 128, 128))


def transform(own_waves, arrived, vertical, legendre, lev, block=128):
    slots, sides, rows, pairs = legendre.shape
    total, lanes = arrived.shape
    any_space = pl.BlockSpec(memory_space=pl.ANY)
    return pl.pallas_call(
        functools.partial(transform_kernel, lev=lev, block=block, limit=2 * rows),
        out_shape=jax.ShapeDtypeStruct((slots, sides, rows, lanes), jnp.bfloat16),
        in_specs=[
            pl.BlockSpec(memory_space=pltpu.SMEM),
            pl.BlockSpec(memory_space=pltpu.VMEM),
            pl.BlockSpec(memory_space=pltpu.VMEM),
            any_space,
        ],
        out_specs=any_space,
        scratch_shapes=[
            pltpu.VMEM((slots, sides, rows, pairs), jnp.bfloat16),
            pltpu.VMEM((sides, total // lev, lanes), jnp.float32),
            [pltpu.VMEM((pairs, 2 * lanes), jnp.bfloat16)] * sides,
            pltpu.VMEM((slots, sides, rows, lanes), jnp.bfloat16),
            pltpu.SemaphoreType.DMA((slots,)),
            pltpu.SemaphoreType.DMA((slots,)),
        ],
        compiler_params=pltpu.CompilerParams(vmem_limit_bytes=50 * 1024 * 1024),
        name="transform",
    )(own_waves, arrived, vertical, legendre)


def body(fourier, vertical_band, cycle_points, legendre, wave_of_slot):
    slots = legendre.shape[0]
    lat, lev = lax.axis_size("lat"), lax.axis_size("lev")
    outgoing = pack(fourier, cycle_points, wave_of_slot, lev, slots)
    split = outgoing.reshape(lat * lev, outgoing.shape[0] // (lat * lev * 4), 4, outgoing.shape[1])
    arrived = lax.all_to_all(split, ("lev", "lat"), split_axis=0, concat_axis=0, tiled=True)
    vertical_band, waves = lax.optimization_barrier((vertical_band, wave_of_slot, outgoing))[:2]
    own_waves = lax.dynamic_slice_in_dim(waves, lax.axis_index(("lat", "lev")) * slots, slots)
    vertical = vertical_matrix(vertical_band, lev)
    return transform(own_waves, arrived.reshape(outgoing.shape), vertical, legendre, lev, lat * lev)


def solution(mesh):
    in_specs = (
        P("lat", None, None, "lev", None),
        P(),
        P("lat"),
        P(("lat", "lev"), None, None, None),
        P(),
    )
    out_specs = P(("lat", "lev"), None, None, None)
    return jax.shard_map(body, mesh=mesh, in_specs=in_specs, out_specs=out_specs, check_vma=False)
```

```python
import functools

import jax
import jax.numpy as jnp
import numpy as np
from jax import lax
from jax.experimental import pallas as pl
from jax.experimental.pallas import tpu as pltpu
from jax.sharding import PartitionSpec as P

NT_DIMS = (((1,), (1,)), ((), ()))


def pack_kernel(cycles_ref, fourier_ref, wave_ref, out_ref,
                fourier, wave, pick, column_ref, rows_ref, packed, in_sem, wave_sem, out_sem, *, lev, slots):
    pairs, parts, waves = fourier_ref.shape[0], 2, fourier_ref.shape[2] // 2
    holders = waves // slots
    lat = holders // lev
    run = pairs * slots
    group = 2

    arrive = pltpu.make_async_copy(fourier_ref, fourier, in_sem)
    arrive.start()
    arrive_wave = pltpu.make_async_copy(wave_ref, wave, wave_sem)
    arrive_wave.start()
    arrive_wave.wait()
    shape = (waves // 128, 128)
    slot = lax.rem(lax.broadcasted_iota(jnp.int32, shape, 0) * 128 + lax.broadcasted_iota(jnp.int32, shape, 1), slots)
    dealt = jnp.max(jnp.abs(lax.shift_right_logical(wave[...], 7) - slot)) == 0
    for i in range(waves // 128):
        column_ref[pl.ds(i * 128, 128), :] = jnp.broadcast_to(wave[pl.ds(i, 1), :], (128, 128)).T
    lane = lax.broadcasted_iota(jnp.int32, (lat, 128), 1)

    def fill(blocks_of):
        for q in range(slots):
            for v in range(lev):
                column = column_ref[pl.ds(v * slots + q, lat, stride=lev * slots), :]
                for b in blocks_of(q):
                    hit = jnp.where(column == lane + b * 128, 1.0, 0.0).astype(jnp.bfloat16)
                    pick[pl.ds((q * lev + v) * lat, lat), pl.ds(b * 128, 128)] = hit

    index = lax.broadcasted_iota(jnp.int32, (1, waves), 1)

    def gather(columns_of):
        arrive.wait()
        for j in range(0, pairs, group):
            blocks = []
            for i in range(j, j + group):
                keep = 2 * index < cycles_ref[i]
                for r in range(parts):
                    part = fourier[i, :, pl.ds(r * waves, waves)]
                    blocks.append(jnp.where(keep, part, jnp.zeros_like(part)))
            block = jnp.concatenate(blocks, axis=0)
            for q in range(slots):
                first, last = columns_of(q)
                picked = lax.dot_general(
                    pick[pl.ds(q * holders, holders), first:last], block[:, first:last], NT_DIMS,
                    preferred_element_type=jnp.float32,
                )
                for i in range(group):
                    rows_ref[pl.ds((j + i) * slots + q, holders, stride=run), :] = picked[:, i * 128:(i + 1) * 128]

    @pl.when(dealt)
    def _():
        fill(lambda q: [q])
        gather(lambda q: (q * 128, (q + 1) * 128))

    @pl.when(jnp.logical_not(dealt))
    def _():
        fill(lambda q: range(waves // 128))
        gather(lambda q: (0, waves))

    part = packed.shape[0] // out_sem.shape[0]

    def leaving(i):
        at = pl.ds(i * part, part)
        return pltpu.make_async_copy(packed.at[at], out_ref.at[at], out_sem.at[i])

    for i in range(out_sem.shape[0]):
        packed[pl.ds(i * part, part), :] = rows_ref[pl.ds(i * part, part), :].astype(jnp.bfloat16)
        leaving(i).start()
    for i in range(out_sem.shape[0]):
        leaving(i).wait()


def split_bf16(value):
    high = value.astype(jnp.bfloat16)
    low = (value - high.astype(jnp.float32)).astype(jnp.bfloat16)
    return high, low


def transform_kernel(wave_ref, arrived, vertical, table_ref, out_ref,
                     tables, folded, right, result, table_sem, out_sem, *, lev, block, limit):
    slots, sides, rows, pairs = tables.shape
    half = arrived.shape[0] // lev
    step = half // 8
    tile = 128

    def table(q, n):
        part = pl.ds(0, n * tile)
        return pltpu.make_async_copy(table_ref.at[q, :, part], tables.at[q, :, part], table_sem.at[q])

    def leaving(q, s):
        return pltpu.make_async_copy(result.at[q, s], out_ref.at[q, s], out_sem.at[q, s])

    def fold():
        for at in range(0, half, step):
            source = jnp.concatenate([arrived[pl.ds(v * half + at, step), :] for v in range(lev)] * 2, axis=1)
            made = jnp.dot(source, vertical[...], preferred_element_type=jnp.float32)
            for s in range(sides):
                folded[s, pl.ds(at, step), :] = made[:, s * 128:(s + 1) * 128]

    degree = 2 * lax.broadcasted_iota(jnp.int32, (rows, 128), 0)

    def prepare(q, s):
        column = folded[s, pl.ds(q, pairs, stride=slots), :]
        right[s][...] = jnp.concatenate(split_bf16(column), axis=1)

    def multiply(q, s, n):
        size = n * tile
        for at in range(0, n * tile, size):
            part = pl.ds(at, size)
            both = jnp.dot(tables[q, s, part], right[s][...], preferred_element_type=jnp.float32)
            product = both[:, :128] + both[:, 128:]
            valid = degree[:size] < limit - 2 * at - s - wave_ref[q]
            result[q, s, part] = jnp.where(valid, product, 0.0).astype(jnp.bfloat16)
        if n * tile < rows:
            result[q, s, pl.ds(n * tile, rows - n * tile)] = jnp.zeros((rows - n * tile, 128), jnp.bfloat16)

    counts = [min(rows // tile, -(-(limit - q * block) // (2 * tile))) for q in range(slots)]
    fits = wave_ref[0] >= 0
    for q in range(1, slots):
        fits = jnp.logical_and(fits, wave_ref[q] >= q * block)
    groups = {0: (0,), 1: (1, 2), 3: (3, 4, 5)}

    @pl.when(fits)
    def _():
        for q in range(slots):
            table(q, counts[q]).start()
        fold()
        prepare(0, 0)
        for q in range(slots):
            for k in groups.get(q, ()):
                table(k, counts[k]).wait()
            for s in range(sides):
                after = q + (s + 1) // sides
                if after < slots:
                    prepare(after, (s + 1) % sides)
                multiply(q, s, counts[q])
                leaving(q, s).start()
        for q in range(slots):
            for s in range(sides):
                leaving(q, s).wait()

    @pl.when(jnp.logical_not(fits))
    def _():
        for q in range(slots):
            table(q, rows // tile).start()
        fold()

        @pl.loop(0, slots)
        def _(q):
            table(q, rows // tile).wait()
            for s in range(sides):
                prepare(q, s)
                multiply(q, s, rows // tile)
                leaving(q, s).start()

        for q in range(slots):
            for s in range(sides):
                leaving(q, s).wait()


def vertical_matrix(band, lev):
    fields, levels, width = band.shape
    reach = (width - 1) // 2
    here = levels // lev
    source = band.reshape(fields, lev, here, width).transpose(1, 0, 2, 3)[:, None, None]
    source = jnp.broadcast_to(source, (lev, 2, 2, fields, here, width)).reshape(-1, width)
    row = np.arange(source.shape[0])[:, None]
    column = np.arange(source.shape[0])[None, :]
    row_level = row // (4 * fields * here) * here + row % here
    row_group = row // (2 * fields * here) % 2 * fields + row // here % fields
    group = column % 2 * fields + column // (2 * levels) % fields
    offset = np.where(row_group == group, column // 2 % levels - row_level + reach, width).astype(np.int8)
    sign = np.where((row // (here * fields) % 2 == 1) & (column // (2 * levels * fields) == 1), -1, 1).astype(np.int8)
    value = jnp.zeros(offset.shape, jnp.float32)
    for d in range(width):
        value = jnp.where(offset == d, source[:, d:d + 1], value)
    value = value * sign
    high = lax.reduce_precision(value, 8, 7)
    return jnp.concatenate([high, value - high], axis=0).astype(jnp.bfloat16)


def pack(fourier, cycle_points, wave_of_slot, lev, slots):
    pairs, sides, fields, here, columns = fourier.shape
    waves = columns // 2
    lanes = sides * fields * here
    any_space = pl.BlockSpec(memory_space=pl.ANY)
    return pl.pallas_call(
        functools.partial(pack_kernel, lev=lev, slots=slots),
        out_shape=jax.ShapeDtypeStruct((waves * pairs, 2 * lanes), jnp.bfloat16),
        in_specs=[pl.BlockSpec(memory_space=pltpu.SMEM), any_space, any_space],
        out_specs=any_space,
        scratch_shapes=[
            pltpu.VMEM((pairs, lanes, columns), jnp.bfloat16),
            pltpu.VMEM((waves // 128, 128), jnp.int32),
            pltpu.VMEM((waves, waves), jnp.bfloat16),
            pltpu.VMEM((waves, 128), jnp.int32),
            pltpu.VMEM((waves * pairs, 2 * lanes), jnp.float32),
            pltpu.VMEM((waves * pairs, 2 * lanes), jnp.bfloat16),
            pltpu.SemaphoreType.DMA,
            pltpu.SemaphoreType.DMA,
            pltpu.SemaphoreType.DMA((2,)),
        ],
        compiler_params=pltpu.CompilerParams(vmem_limit_bytes=60 * 1024 * 1024),
        name="pack",
    )(cycle_points, fourier.reshape(pairs, lanes, columns), wave_of_slot.reshape(waves // 128, 128))


def transform(own_waves, arrived, vertical, legendre, lev, block=128):
    slots, sides, rows, pairs = legendre.shape
    total, lanes = arrived.shape
    any_space = pl.BlockSpec(memory_space=pl.ANY)
    return pl.pallas_call(
        functools.partial(transform_kernel, lev=lev, block=block, limit=2 * rows),
        out_shape=jax.ShapeDtypeStruct((slots, sides, rows, lanes), jnp.bfloat16),
        in_specs=[
            pl.BlockSpec(memory_space=pltpu.SMEM),
            pl.BlockSpec(memory_space=pltpu.VMEM),
            pl.BlockSpec(memory_space=pltpu.VMEM),
            any_space,
        ],
        out_specs=any_space,
        scratch_shapes=[
            pltpu.VMEM((slots, sides, rows, pairs), jnp.bfloat16),
            pltpu.VMEM((sides, total // lev, lanes), jnp.float32),
            [pltpu.VMEM((pairs, 2 * lanes), jnp.bfloat16)] * sides,
            pltpu.VMEM((slots, sides, rows, lanes), jnp.bfloat16),
            pltpu.SemaphoreType.DMA((slots,)),
            pltpu.SemaphoreType.DMA((slots, sides)),
        ],
        compiler_params=pltpu.CompilerParams(vmem_limit_bytes=50 * 1024 * 1024),
        name="transform",
    )(own_waves, arrived, vertical, legendre)


def body(fourier, vertical_band, cycle_points, legendre, wave_of_slot):
    slots = legendre.shape[0]
    lat, lev = lax.axis_size("lat"), lax.axis_size("lev")
    outgoing = pack(fourier, cycle_points, wave_of_slot, lev, slots)
    split = outgoing.reshape(lat * lev, outgoing.shape[0] // (lat * lev * 4), 4, outgoing.shape[1])
    arrived = lax.all_to_all(split, ("lev", "lat"), split_axis=0, concat_axis=0, tiled=True)
    vertical_band, waves = lax.optimization_barrier((vertical_band, wave_of_slot, outgoing))[:2]
    own_waves = lax.dynamic_slice_in_dim(waves, lax.axis_index(("lat", "lev")) * slots, slots)
    vertical = vertical_matrix(vertical_band, lev)
    return transform(own_waves, arrived.reshape(outgoing.shape), vertical, legendre, lev, lat * lev)


def solution(mesh):
    in_specs = (
        P("lat", None, None, "lev", None),
        P(),
        P("lat"),
        P(("lat", "lev"), None, None, None),
        P(),
    )
    out_specs = P(("lat", "lev"), None, None, None)
    return jax.shard_map(body, mesh=mesh, in_specs=in_specs, out_specs=out_specs, check_vma=False)
```
